32 devices in a mesh: dom: 4 (over x, core), ctx: 8 (over z, y).
Axes of the slice: x: 2, y: 2, z: 4, core: 2. Of those that a mesh axis runs over, the one named last changes fastest.
Arguments:
- prompt_kv: bfloat16 [16384, 1024], P('ctx'), may hold values from -6 to 6
- suffix_kv: bfloat16 [32, 12, 1024], P('dom'), may hold values from -12 to 12
- new_kv: bfloat16 [4, 32, 1024], P(None, 'dom'), may hold values from -12 to 12
- queries: bfloat16 [4, 32, 4096], P(None, 'dom', 'ctx'), may hold values from -128 to 128
- ancestors: int32 [4, 32], P(None, 'dom'), may hold values from 0 to 31, as said below
Outputs:
- attended: float32 [4, 32, 4096], P(None, 'dom', 'ctx')
- suffix_out: bfloat16 [32, 16, 1024], P('dom')
The draws below stay inside these ranges and needn't reach their ends.
Inputs may be any that keep to these rules, and one draw needn't show every extreme that they name: ancestors[s, p] differs from p by at most 4, and by exactly 4 for some particle of every step.
All inputs are finite; a program needn't handle non-finite values.
Results may differ from the reference program's by a relative error of at most 0.0049.
Values may be sent and summed in bfloat16 or wider, within the bound.
A program may use at most 128 MiB of HBM per device.

```python
import jax
import jax.numpy as jnp
from jax import lax

HEADS = 32
KV_HEADS = 4
HEAD_DIM = 128
GROUP = 8
P_DEV = 8
HIST = 12
STEPS = 4
SUF = 16
REACH = 4
PARTICLES = 32
CONTEXT = 16384
N_DOM = 4


def shared_prompt(key):
    key_width = KV_HEADS * HEAD_DIM
    base = jnp.clip(jax.random.normal(jax.random.fold_in(key, 11), (CONTEXT, 2 * key_width), jnp.float32), -6.0, 6.0)
    picks = jax.random.randint(jax.random.fold_in(key, 12), (STEPS, PARTICLES, HEADS), 0, CONTEXT - 1).astype(jnp.int32)
    flat = picks.reshape(-1)
    target = base[flat + 1, :key_width]
    mixed = target
    base = base.at[flat + 1, :key_width].set(mixed)
    return base


def draw_prompt_kv(key, part):
    base = shared_prompt(key)
    return base.astype(jnp.bfloat16)


def draw_queries(key, part):
    blend = 0.0
    key = jax.random.fold_in(key, 5)
    shape = (STEPS, PARTICLES, HEADS, HEAD_DIM)
    noise = jnp.clip(2.5 * jax.random.normal(jax.random.fold_in(key, 1), shape, jnp.float32), -15.0, 15.0)
    particle_index = jnp.arange(PARTICLES)[None, :, None, None]
    head_index = jnp.arange(HEADS)[None, None, :, None]
    chosen = ((particle_index % 5 == 0) & (head_index % 4 == 0)).astype(jnp.float32) * blend
    values = noise * (1.0 - chosen)
    return values.reshape(STEPS, PARTICLES, HEADS * HEAD_DIM).astype(jnp.bfloat16)


def draw_ancestors(key, part):
    key = jax.random.fold_in(key, 7)
    offsets = jax.random.randint(key, (STEPS, PARTICLES), -REACH, REACH + 1).astype(jnp.int32)
    index = jnp.arange(PARTICLES, dtype=jnp.int32)[None, :]
    parent = jnp.clip(index + offsets, 0, PARTICLES - 1)
    parent = parent.at[:, REACH].set(0)
    parent = parent.at[:, PARTICLES - 1 - REACH].set(PARTICLES - 1)
    return parent.astype(jnp.int32)


def level_of(rng, extent, pieces, low, largest):
    def one(position, parts):
        steps = jax.random.uniform(jax.random.fold_in(jax.random.fold_in(rng, 6), position), (parts,), jnp.float32, low / len(pieces), largest / len(pieces))
        return jnp.repeat(jnp.exp(steps), extent[position] // parts).reshape((-1,) + (1,) * (len(extent) - position - 1))

    level = one(*pieces[0])
    for cut in pieces[1:]:
        level = level * one(*cut)
    return level


def gaussian(own_key, shape, width, limit, pieces=(), held_as=jnp.bfloat16):
    factor_of = level_of(own_key, shape, pieces, -0.22, 0.18) if pieces else 1.0
    entries = jax.random.normal(own_key, shape, jnp.float32) * width * factor_of
    return jnp.minimum(jnp.maximum(entries, -limit), limit).astype(held_as)


def setup_inputs(seed: int = 0) -> dict:
    arg_keys = jax.random.split(jax.random.key(seed), 6)
    prompt_kv = draw_prompt_kv(jax.random.fold_in(arg_keys[5], 71), 0)
    suffix_kv = gaussian(arg_keys[1], (PARTICLES, HIST, 2 * KV_HEADS * HEAD_DIM), 2.0, 12.0, ((0, 4),))
    new_kv = gaussian(arg_keys[2], (STEPS, PARTICLES, 2 * KV_HEADS * HEAD_DIM), 2.0, 12.0, ((1, 4),))
    queries = draw_queries(jax.random.fold_in(arg_keys[5], 71), 0)
    ancestors = draw_ancestors(jax.random.fold_in(arg_keys[5], 71), 0)
    return dict(prompt_kv=prompt_kv, suffix_kv=suffix_kv, new_kv=new_kv, queries=queries, ancestors=ancestors)


floor_score = -1e30


def reference(prompt_kv, suffix_kv, new_kv, queries, ancestors):
    key_width = KV_HEADS * HEAD_DIM
    inverse_root = 1.0 / (HEAD_DIM ** 0.5)
    cache = jnp.concatenate([suffix_kv, jnp.zeros((PARTICLES, STEPS, 2 * key_width), jnp.bfloat16)], axis=1)
    prompt_keys = prompt_kv[:, :key_width].astype(jnp.float32).reshape(CONTEXT, KV_HEADS, HEAD_DIM)
    prompt_vals = prompt_kv[:, key_width:].astype(jnp.float32).reshape(CONTEXT, KV_HEADS, HEAD_DIM)
    outputs = []
    for moment in range(STEPS):
        cache = cache.at[:, HIST + moment, :].set(new_kv[moment])
        valid = jnp.arange(SUF) <= HIST + moment
        query_blocks = queries[moment].reshape(N_DOM, P_DEV, KV_HEADS, GROUP, HEAD_DIM)
        cache_blocks = cache.reshape(N_DOM, P_DEV, SUF, 2 * key_width)

        def attend(pair):
            query_part, cache_part = pair
            query_wide = query_part.astype(jnp.float32)
            suffix_keys = cache_part[:, :, :key_width].astype(jnp.float32).reshape(P_DEV, SUF, KV_HEADS, HEAD_DIM)
            suffix_vals = cache_part[:, :, key_width:].astype(jnp.float32).reshape(P_DEV, SUF, KV_HEADS, HEAD_DIM)
            prompt_score = jnp.einsum("pged,tgd->pget", query_wide, prompt_keys) * inverse_root
            suffix_score = jnp.einsum("pged,psgd->pges", query_wide, suffix_keys) * inverse_root
            suffix_score = jnp.where(valid, suffix_score, floor_score)
            peak = jnp.maximum(prompt_score.max(-1), suffix_score.max(-1))
            prompt_weight = jnp.exp(prompt_score - peak[..., None])
            suffix_weight = jnp.exp(suffix_score - peak[..., None])
            total = prompt_weight.sum(-1) + suffix_weight.sum(-1)
            prompt_round = lax.optimization_barrier(prompt_weight.astype(jnp.bfloat16)).astype(jnp.float32)
            suffix_round = lax.optimization_barrier(suffix_weight.astype(jnp.bfloat16)).astype(jnp.float32)
            summed = jnp.einsum("pget,tgd->pged", prompt_round, prompt_vals)
            summed = summed + jnp.einsum("pges,psgd->pged", suffix_round, suffix_vals)
            return (summed / total[..., None]).reshape(P_DEV, HEADS * HEAD_DIM)

        result = lax.map(attend, (query_blocks, cache_blocks))
        outputs.append(result.reshape(PARTICLES, HEADS * HEAD_DIM))
        cache = cache[ancestors[moment]]
    return jnp.stack(outputs), cache
```

```python
import functools

import jax
import jax.numpy as jnp
from jax import lax
from jax.experimental import pallas as pl
from jax.experimental.pallas import tpu as pltpu
from jax.sharding import PartitionSpec as P

HEADS = 32
HEAD_DIM = 128
MESH = pl.DeviceIdType.MESH
LOG2E = 1.4426950408889634
FLOOR = -1e30
LANES = 128
SPAN = 2
FAR = (-1, 1, -2, 2)


def nt(a, b):
    return lax.dot_general(a, b, (((1,), (1,)), ((), ())), preferred_element_type=jnp.float32)


def nn(a, b):
    return jnp.dot(a, b, preferred_element_type=jnp.float32)


def kernel(
    n_ctx, n_dom, key_heads, steps, history,
    kv_ref, cache_ref, q_ref, anc_ref,
    att_ref, out_ref,
    k_buf, v_buf, q_all, part, got, window, anc_win,
    kv_sem, q_send, q_recv, p_send, p_recv, w_send, w_recv, a_send, a_recv,
):
    column = lax.axis_index("ctx")
    row = lax.axis_index("dom")
    own = HEADS // n_ctx
    members = n_ctx // key_heads
    my_head = column // members
    my_member = column % members
    parts = q_ref.shape[1]
    slots = history + steps
    moments = steps * parts
    rows = own * moments
    key_width = key_heads * HEAD_DIM
    factor = LOG2E / HEAD_DIM**0.5

    def head_at(i):
        return lax.rem(my_head + i, key_heads)

    def loads(i):
        e = head_at(i)
        at = pl.multiple_of(e * HEAD_DIM, HEAD_DIM)
        return (
            pltpu.make_async_copy(kv_ref.at[:, pl.ds(at, HEAD_DIM)], k_buf.at[i], kv_sem.at[i, 0]),
            pltpu.make_async_copy(
                kv_ref.at[:, pl.ds(at + key_width, HEAD_DIM)], v_buf.at[i], kv_sem.at[i, 1]
            ),
        )

    for i in range(key_heads):
        for copy in loads(i):
            copy.start()

    barrier = pltpu.get_barrier_semaphore()
    for o in range(1, n_ctx):
        pl.semaphore_signal(
            barrier, inc=1, device_id={"ctx": lax.rem(column + o, n_ctx)}, device_id_type=MESH
        )

    def inside(delta):
        return (row + delta >= 0) & (row + delta < n_dom)

    for delta in FAR:
        @pl.when(inside(delta))
        def _():
            pl.semaphore_signal(barrier, inc=1, device_id={"dom": row + delta}, device_id_type=MESH)

    wide = jnp.concatenate([q_ref[s].astype(jnp.float32) for s in range(steps)], axis=0)
    mine = jnp.concatenate(
        [wide[:, h * HEAD_DIM : (h + 1) * HEAD_DIM] for h in range(own)], axis=0
    ).astype(jnp.bfloat16)
    q_all[column] = mine
    lane = lax.broadcasted_iota(jnp.int32, (steps, LANES), 1)
    tile = jnp.full((steps, LANES), -1, jnp.int32)
    anc = anc_ref[...]
    for p in range(parts):
        tile = jnp.where(lane == lax.rem(row * parts + p, LANES), anc[:, p : p + 1], tile)
    anc_win[SPAN] = jnp.concatenate([tile, jnp.full((8 - steps, LANES), -1, jnp.int32)], axis=0)
    for delta in FAR:
        @pl.when(jnp.logical_not(inside(delta)))
        def _():
            anc_win[SPAN + delta] = jnp.full((8, LANES), -1, jnp.int32)
            window[SPAN + delta] = jnp.zeros(window.shape[1:], window.dtype)

    near = jnp.minimum(row, SPAN) + jnp.minimum(n_dom - 1 - row, SPAN)
    pl.semaphore_wait(barrier, n_ctx - 1 + near)

    def q_copy(peer, source):
        return pltpu.make_async_remote_copy(
            src_ref=q_all.at[source], dst_ref=q_all.at[source],
            send_sem=q_send.at[peer], recv_sem=q_recv.at[source],
            device_id={"ctx": peer}, device_id_type=MESH,
        )

    def peers_of(i):
        e = lax.rem(my_head + key_heads - i, key_heads)
        first = 1 if i == 0 else 0
        return [e * members + lax.rem(my_member + o, members) for o in range(first, members)]

    for i in range(key_heads):
        for peer in peers_of(i):
            q_copy(peer, column).start()

    def w_copy(delta):
        return pltpu.make_async_remote_copy(
            src_ref=cache_ref, dst_ref=window.at[SPAN - delta],
            send_sem=w_send.at[SPAN + delta], recv_sem=w_recv.at[SPAN - delta],
            device_id={"dom": row + delta}, device_id_type=MESH,
        )

    def a_copy(delta):
        return pltpu.make_async_remote_copy(
            src_ref=anc_win.at[SPAN], dst_ref=anc_win.at[SPAN - delta],
            send_sem=a_send.at[SPAN + delta], recv_sem=a_recv.at[SPAN - delta],
            device_id={"dom": row + delta}, device_id_type=MESH,
        )

    def w_arrival(delta):
        return pltpu.make_async_remote_copy(
            src_ref=cache_ref, dst_ref=window.at[SPAN + delta],
            send_sem=w_send.at[SPAN - delta], recv_sem=w_recv.at[SPAN + delta],
            device_id={"dom": row + delta}, device_id_type=MESH,
        )

    def a_arrival(delta):
        return pltpu.make_async_remote_copy(
            src_ref=anc_win.at[SPAN], dst_ref=anc_win.at[SPAN + delta],
            send_sem=a_send.at[SPAN - delta], recv_sem=a_recv.at[SPAN + delta],
            device_id={"dom": row + delta}, device_id_type=MESH,
        )

    for delta in FAR:
        @pl.when(inside(delta))
        def _():
            a_copy(delta).start()
            w_copy(delta).start()

    window[SPAN] = cache_ref[...]

    def p_copy(peer, source):
        return pltpu.make_async_remote_copy(
            src_ref=part.at[peer], dst_ref=got.at[source],
            send_sem=p_send.at[peer], recv_sem=p_recv.at[source],
            device_id={"ctx": peer}, device_id_type=MESH,
        )

    def stats_tile(m, l):
        n = m.shape[0]
        li = lax.broadcasted_iota(jnp.int32, (n, LANES), 1)
        both = jnp.where(li == 0, m, jnp.where(li == 1, l, 0.0))
        turned = jnp.transpose(both)[:8]
        if n < LANES:
            turned = jnp.concatenate([turned, jnp.zeros((8, LANES - n), jnp.float32)], axis=1)
        return turned

    for i in range(key_heads):
        e = head_at(i)
        for copy in loads(i):
            copy.wait()
        for o in range(1 if i == 0 else 0, members):
            source = e * members + lax.rem(my_member + o, members)
            q_copy(source, source).wait_recv()
        q = q_all[pl.ds(e * members, members)].reshape(members * rows, HEAD_DIM)
        score = nt(q, k_buf[i])
        peak = jnp.max(score, axis=1, keepdims=True) * factor
        weight = jnp.exp2(score * factor - peak)
        total = jnp.sum(weight, axis=1, keepdims=True)
        summed = nn(weight.astype(jnp.bfloat16), v_buf[i])
        for m in range(members):
            peer = e * members + m
            cut = slice(m * rows, (m + 1) * rows)
            part[peer, :rows] = summed[cut]
            part[peer, rows:] = stats_tile(peak[cut], total[cut])
            if i == 0:
                @pl.when(m != my_member)
                def _():
                    p_copy(peer, column).start()
            else:
                p_copy(peer, column).start()

    for delta in FAR:
        @pl.when(inside(delta))
        def _():
            a_arrival(delta).wait_recv()
    known = anc_win[0]
    for w in range(1, 2 * SPAN + 1):
        known = jnp.maximum(known, anc_win[w])
    known = jnp.where(known >= 0, lax.rem(known, LANES), -1)
    q_id = lax.broadcasted_iota(jnp.int32, (LANES, LANES), 0)
    one = lax.broadcasted_iota(jnp.int32, (parts, LANES), 1) == lax.rem(
        row * parts + lax.broadcasted_iota(jnp.int32, (parts, LANES), 0), LANES
    )
    one = one.astype(jnp.float32)
    zero = jnp.zeros_like(one)
    origin = {}
    for k in range(steps - 1, -1, -1):
        origin[k, k] = one
        start = [origin[s, k + 1] for s in range(k + 1, steps + 1) if s != k + 1] + [one]
        names = list(range(k + 2, steps + 1)) + [k + 1]
        turn = (known[k : k + 1, :] == q_id).astype(jnp.float32).astype(jnp.bfloat16)
        moved = nt(jnp.concatenate(start, axis=0).astype(jnp.bfloat16), turn)
        for n, s in enumerate(names):
            origin[s, k] = moved[n * parts : (n + 1) * parts]
    stack = jnp.concatenate(
        [origin.get((s, k), zero) if s >= k else zero for k in range(steps) for s in range(steps + 1)],
        axis=0,
    ).astype(jnp.bfloat16)
    cols = (2 * SPAN + 1) * parts * slots
    block = (steps + 1) * parts
    col = lax.broadcasted_iota(jnp.int32, (LANES, cols), 1)
    particle = lax.rem((row - SPAN) * parts + col // slots + 16 * LANES, LANES)
    spread = (particle == lax.broadcasted_iota(jnp.int32, (LANES, cols), 0)).astype(
        jnp.float32
    ).astype(jnp.bfloat16)
    from_where = nn(stack, spread)
    slot = lax.rem(lax.broadcasted_iota(jnp.int32, (block, cols), 1), slots)
    kind = jnp.maximum(slot - history, 0)
    valid = jnp.zeros((block, cols), jnp.float32)
    for k in range(steps):
        valid = jnp.where(kind == k, from_where[k * block : (k + 1) * block], valid)

    for delta in FAR:
        @pl.when(inside(delta))
        def _():
            w_arrival(delta).wait_recv()

    pick = jnp.broadcast_to(valid[moments:, None, :], (parts, slots, cols)).reshape(parts * slots, cols)
    same = lax.rem(lax.broadcasted_iota(jnp.int32, (parts * slots, cols), 1), slots) == lax.rem(
        lax.broadcasted_iota(jnp.int32, (parts * slots, cols), 0), slots
    )
    pick = jnp.where(same, pick, 0.0).astype(jnp.bfloat16)
    for c in range(0, 2 * key_width, 256):
        piece = window[:, :, c : c + 256].reshape(cols, 256)
        out_ref[:, c : c + 256] = nn(pick, piece).astype(jnp.bfloat16)

    at = pl.multiple_of(my_head * HEAD_DIM, HEAD_DIM)
    keys = window[:, :, pl.ds(at, HEAD_DIM)].reshape(cols, HEAD_DIM)
    vals = window[:, :, pl.ds(pl.multiple_of(at + key_width, HEAD_DIM), HEAD_DIM)].reshape(
        cols, HEAD_DIM
    )
    allowed = jnp.concatenate([valid[:moments]] * own, axis=0) > 0.5
    score = jnp.where(allowed, nt(q_all[column], keys) * factor, FLOOR)
    peak = jnp.max(score, axis=1, keepdims=True)
    weight = jnp.where(allowed, jnp.exp2(score - peak), 0.0)
    total = jnp.sum(weight, axis=1, keepdims=True)
    summed = nn(weight.astype(jnp.bfloat16), vals)

    for o in range(1, n_ctx):
        source = lax.rem(column + o, n_ctx)
        p_copy(source, source).wait_recv()
    peaks, totals, sums = [peak], [total], [summed]
    for o in range(n_ctx):
        source = lax.rem(column + o, n_ctx)
        whole = part.at[column] if o == 0 else got.at[source]
        stats = jnp.transpose(
            jnp.concatenate([whole[rows:], jnp.zeros((LANES - 8, LANES), jnp.float32)], axis=0)
        )[:rows]
        peaks.append(stats[:, 0:1])
        totals.append(stats[:, 1:2])
        sums.append(whole[:rows])
    highest = functools.reduce(jnp.maximum, peaks)
    bottom, top = 0.0, 0.0
    for m, l, s in zip(peaks, totals, sums):
        scale = jnp.exp2(m - highest)
        bottom = bottom + l * scale
        top = top + s * scale
    result = top / bottom
    for h in range(own):
        for s in range(steps):
            at = h * moments + s * parts
            att_ref[s, :, h * HEAD_DIM : (h + 1) * HEAD_DIM] = result[at : at + parts]

    for o in range(1, n_ctx):
        peer = lax.rem(column + o, n_ctx)
        q_copy(peer, column).wait_send()
        p_copy(peer, column).wait_send()
    for delta in FAR:
        @pl.when(inside(delta))
        def _():
            a_copy(delta).wait_send()
            w_copy(delta).wait_send()


def solution(mesh):
    n_ctx, n_dom = mesh.shape["ctx"], mesh.shape["dom"]

    def shards(prompt_kv, suffix_kv, new_kv, queries, ancestors):
        parts, history, width = suffix_kv.shape
        steps = queries.shape[0]
        key_heads = width // (2 * HEAD_DIM)
        slots = history + steps
        positions = prompt_kv.shape[0]
        own = HEADS // n_ctx
        rows = own * steps * parts
        cache = jnp.concatenate([suffix_kv, jnp.transpose(new_kv, (1, 0, 2))], axis=1)
        cache = cache.reshape(parts * slots, width)
        vmem = pl.BlockSpec(memory_space=pltpu.VMEM)
        dma = pltpu.SemaphoreType.DMA
        attended, suffix_out = pl.pallas_call(
            functools.partial(kernel, n_ctx, n_dom, key_heads, steps, history),
            out_shape=(
                jax.ShapeDtypeStruct((steps, parts, own * HEAD_DIM), jnp.float32),
                jax.ShapeDtypeStruct((parts * slots, width), jnp.bfloat16),
            ),
            in_specs=[pl.BlockSpec(memory_space=pl.ANY), vmem, vmem, vmem],
            out_specs=(vmem, vmem),
            scratch_shapes=[
                pltpu.VMEM((key_heads, positions, HEAD_DIM), jnp.bfloat16),
                pltpu.VMEM((key_heads, positions, HEAD_DIM), jnp.bfloat16),
                pltpu.VMEM((n_ctx, rows, HEAD_DIM), jnp.bfloat16),
                pltpu.VMEM((n_ctx, rows + 8, HEAD_DIM), jnp.float32),
                pltpu.VMEM((n_ctx, rows + 8, HEAD_DIM), jnp.float32),
                pltpu.VMEM((2 * SPAN + 1, parts * slots, width), jnp.bfloat16),
                pltpu.VMEM((2 * SPAN + 1, 8, LANES), jnp.int32),
                dma((key_heads, 2)),
                dma((n_ctx,)), dma((n_ctx,)), dma((n_ctx,)), dma((n_ctx,)),
                dma((2 * SPAN + 1,)), dma((2 * SPAN + 1,)),
                dma((2 * SPAN + 1,)), dma((2 * SPAN + 1,)),
            ],
            compiler_params=pltpu.CompilerParams(
                collective_id=0, has_side_effects=True, vmem_limit_bytes=48 * 1024 * 1024
            ),
            cost_estimate=pl.CostEstimate(
                flops=4 * HEADS * steps * parts * positions * HEAD_DIM,
                bytes_accessed=4 * positions * width,
                transcendentals=HEADS * steps * parts * positions,
            ),
        )(prompt_kv, cache, queries, ancestors)
        return attended, suffix_out.reshape(parts, slots, width)

    return jax.shard_map(
        shards,
        mesh=mesh,
        in_specs=(
            P("ctx", None),
            P("dom", None, None),
            P(None, "dom", None),
            P(None, "dom", "ctx"),
            P(None, "dom"),
        ),
        out_specs=(P(None, "dom", "ctx"), P("dom", None, None)),
        check_vma=False,
    )
```

```python
import functools

import jax
import jax.numpy as jnp
from jax import lax
from jax.experimental import pallas as pl
from jax.experimental.pallas import tpu as pltpu
from jax.sharding import PartitionSpec as P

HEADS = 32
HEAD_DIM = 128
MESH = pl.DeviceIdType.MESH
LOG2E = 1.4426950408889634
FLOOR = -1e30
LANES = 128
CODES = 32767.0
TINY = 1e-30
SPAN = 2
FAR = (-1, 1, -2, 2)


def nt(a, b):
    return lax.dot_general(a, b, (((1,), (1,)), ((), ())), preferred_element_type=jnp.float32)


def nn(a, b):
    return jnp.dot(a, b, preferred_element_type=jnp.float32)


def kernel(
    n_ctx, n_dom, key_heads, steps, history,
    kv_ref, old_ref, new_ref, q_ref, anc_ref,
    att_ref, out_ref,
    k_buf, v_buf, q_raw, anc_raw, q_all, part, got, part_stats, got_stats, window, anc_win,
    kv_sem, in_sem, q_send, q_recv, r_send, p_send, p_recv, t_send, t_recv,
    w_send, w_recv, n_send, n_recv, a_send, a_recv,
):
    column = lax.axis_index("ctx")
    row = lax.axis_index("dom")
    own = HEADS // n_ctx
    members = n_ctx // key_heads
    my_head = column // members
    my_member = column % members
    parts = q_ref.shape[1]
    slots = history + steps
    moments = steps * parts
    rows = own * moments
    key_width = key_heads * HEAD_DIM
    factor = LOG2E / HEAD_DIM**0.5

    pair = column + 1 - 2 * (column % 2)
    order = [0] + sorted(range(1, key_heads), key=lambda i: (i < key_heads // 2, i))

    def head_at(i):
        e, bit = my_head, 1
        while bit < key_heads:
            if i & bit:
                e = e + bit - 2 * bit * (my_head // bit % 2)
            bit *= 2
        return e

    def same_side(i):
        e = head_at(i)
        half = members // 2
        mine = my_member // 2
        first = 1 if i == 0 else 0
        return [
            e * members + 2 * lax.rem(mine + o, half) + my_member % 2 for o in range(first, half)
        ]

    def loads(i):
        e = head_at(i)
        at = pl.multiple_of(e * HEAD_DIM, HEAD_DIM)
        return (
            pltpu.make_async_copy(kv_ref.at[:, pl.ds(at, HEAD_DIM)], k_buf.at[i], kv_sem.at[i, 0]),
            pltpu.make_async_copy(
                kv_ref.at[:, pl.ds(at + key_width, HEAD_DIM)], v_buf.at[i], kv_sem.at[i, 1]
            ),
        )

    q_in = pltpu.make_async_copy(q_ref, q_raw, in_sem.at[0])
    anc_in = pltpu.make_async_copy(anc_ref, anc_raw, in_sem.at[1])
    old_rows, new_rows = old_ref.shape[0], new_ref.shape[0]
    old_in = pltpu.make_async_copy(old_ref, window.at[SPAN, pl.ds(0, old_rows)], in_sem.at[2])
    new_in = pltpu.make_async_copy(
        new_ref, window.at[SPAN, pl.ds(old_rows, new_rows)], in_sem.at[3]
    )
    q_in.start()
    anc_in.start()
    for i in order:
        for copy in loads(i):
            copy.start()
    old_in.start()
    new_in.start()

    barrier = pltpu.get_barrier_semaphore()
    for o in range(1, n_ctx):
        pl.semaphore_signal(
            barrier, inc=1, device_id={"ctx": lax.rem(column + o, n_ctx)}, device_id_type=MESH
        )

    def inside(delta):
        return (row + delta >= 0) & (row + delta < n_dom)

    for delta in FAR:
        @pl.when(inside(delta))
        def _():
            pl.semaphore_signal(barrier, inc=1, device_id={"dom": row + delta}, device_id_type=MESH)

    q_in.wait()
    anc_in.wait()
    wide = jnp.concatenate([q_raw[s].astype(jnp.float32) for s in range(steps)], axis=0)
    mine = jnp.concatenate(
        [wide[:, h * HEAD_DIM : (h + 1) * HEAD_DIM] for h in range(own)], axis=0
    ).astype(jnp.bfloat16)
    q_all[column] = mine
    lane = lax.broadcasted_iota(jnp.int32, (steps, LANES), 1)
    tile = jnp.full((steps, LANES), -1, jnp.int32)
    anc = anc_raw[...]
    for p in range(parts):
        tile = jnp.where(lane == lax.rem(row * parts + p, LANES), anc[:, p : p + 1], tile)
    anc_win[SPAN] = jnp.concatenate([tile, jnp.full((8 - steps, LANES), -1, jnp.int32)], axis=0)
    for delta in FAR:
        @pl.when(jnp.logical_not(inside(delta)))
        def _():
            anc_win[SPAN + delta] = jnp.full((8, LANES), -1, jnp.int32)
            window[SPAN + delta] = jnp.zeros(window.shape[1:], window.dtype)

    near = jnp.minimum(row, SPAN) + jnp.minimum(n_dom - 1 - row, SPAN)
    pl.semaphore_wait(barrier, n_ctx - 1 + near)

    def q_copy(peer, source, sems):
        return pltpu.make_async_remote_copy(
            src_ref=q_all.at[source], dst_ref=q_all.at[source],
            send_sem=sems, recv_sem=q_recv.at[source],
            device_id={"ctx": peer}, device_id_type=MESH,
        )

    def relay(i):
        for source in same_side(i):
            q_copy(source, source, q_send.at[source]).wait_recv()
            q_copy(pair, source, r_send.at[source]).start()

    q_copy(pair, column, r_send.at[column]).start()
    for i in order:
        for peer in same_side(i):
            q_copy(peer, column, q_send.at[peer]).start()

    def w_pieces(delta, at, sent, landed):
        return [
            pltpu.make_async_remote_copy(
                src_ref=source, dst_ref=window.at[SPAN + at, pl.ds(first, source.shape[0])],
                send_sem=send.at[SPAN + sent], recv_sem=recv.at[SPAN + landed],
                device_id={"dom": row + delta}, device_id_type=MESH,
            )
            for source, first, send, recv in (
                (old_ref, 0, w_send, w_recv), (new_ref, old_rows, n_send, n_recv)
            )
        ]

    def w_copies(delta):
        return w_pieces(delta, -delta, delta, -delta)

    def w_arrivals(delta):
        return w_pieces(delta, delta, -delta, delta)

    def a_copy(delta):
        return pltpu.make_async_remote_copy(
            src_ref=anc_win.at[SPAN], dst_ref=anc_win.at[SPAN - delta],
            send_sem=a_send.at[SPAN + delta], recv_sem=a_recv.at[SPAN - delta],
            device_id={"dom": row + delta}, device_id_type=MESH,
        )

    def a_arrival(delta):
        return pltpu.make_async_remote_copy(
            src_ref=anc_win.at[SPAN], dst_ref=anc_win.at[SPAN + delta],
            send_sem=a_send.at[SPAN - delta], recv_sem=a_recv.at[SPAN + delta],
            device_id={"dom": row + delta}, device_id_type=MESH,
        )

    for delta in FAR:
        @pl.when(inside(delta))
        def _():
            a_copy(delta).start()
            for copy in w_copies(delta):
                copy.start()

    def p_copies(peer, source):
        return [
            pltpu.make_async_remote_copy(
                src_ref=mine.at[peer], dst_ref=theirs.at[source],
                send_sem=send.at[peer], recv_sem=recv.at[source],
                device_id={"ctx": peer}, device_id_type=MESH,
            )
            for mine, theirs, send, recv in (
                (part_stats, got_stats, t_send, t_recv), (part, got, p_send, p_recv)
            )
        ]

    def stats_tile(*columns):
        n = columns[0].shape[0]
        li = lax.broadcasted_iota(jnp.int32, (n, LANES), 1)
        both = jnp.zeros((n, LANES), jnp.float32)
        for at, value in enumerate(columns):
            both = jnp.where(li == at, value, both)
        turned = jnp.transpose(both)[:8]
        if n < LANES:
            turned = jnp.concatenate([turned, jnp.zeros((8, LANES - n), jnp.float32)], axis=1)
        return turned

    relay(0)
    relay(order[1])
    for n, i in enumerate(order):
        e = head_at(i)
        for copy in loads(i):
            copy.wait()
        for o in range(members // 2):
            source = e * members + 2 * o + pair % 2
            q_copy(source, source, q_send.at[source]).wait_recv()
        q = q_all[pl.ds(e * members, members)].reshape(members * rows, HEAD_DIM)
        score = nt(q, k_buf[i])
        peak = jnp.max(score, axis=1, keepdims=True) * factor
        weight = jnp.exp2(score * factor - peak)
        total = jnp.sum(weight, axis=1, keepdims=True)
        summed = nn(weight.astype(jnp.bfloat16), v_buf[i])
        largest = jnp.max(jnp.abs(summed), axis=1, keepdims=True)
        coded = jnp.round(summed * (CODES / jnp.maximum(largest, TINY))).astype(jnp.int32)
        coded = coded.astype(jnp.int16)
        for m in range(members):
            peer = e * members + m
            cut = slice(m * rows, (m + 1) * rows)
            part[peer] = coded[cut]
            part_stats[peer] = stats_tile(peak[cut], total[cut], largest[cut])
            if i == 0:
                @pl.when(m != my_member)
                def _():
                    for copy in p_copies(peer, column):
                        copy.start()
            else:
                for copy in p_copies(peer, column):
                    copy.start()
        if n == 0:
            for later in order[2:]:
                relay(later)

    for delta in FAR:
        @pl.when(inside(delta))
        def _():
            a_arrival(delta).wait_recv()
    known = anc_win[0]
    for w in range(1, 2 * SPAN + 1):
        known = jnp.maximum(known, anc_win[w])
    known = jnp.where(known >= 0, lax.rem(known, LANES), -1)
    q_id = lax.broadcasted_iota(jnp.int32, (LANES, LANES), 0)
    one = lax.broadcasted_iota(jnp.int32, (parts, LANES), 1) == lax.rem(
        row * parts + lax.broadcasted_iota(jnp.int32, (parts, LANES), 0), LANES
    )
    one = one.astype(jnp.float32)
    zero = jnp.zeros_like(one)
    origin = {}
    for k in range(steps - 1, -1, -1):
        origin[k, k] = one
        start = [origin[s, k + 1] for s in range(k + 1, steps + 1) if s != k + 1] + [one]
        names = list(range(k + 2, steps + 1)) + [k + 1]
        turn = (known[k : k + 1, :] == q_id).astype(jnp.float32).astype(jnp.bfloat16)
        moved = nt(jnp.concatenate(start, axis=0).astype(jnp.bfloat16), turn)
        for n, s in enumerate(names):
            origin[s, k] = moved[n * parts : (n + 1) * parts]
    stack = jnp.concatenate(
        [origin.get((s, k), zero) if s >= k else zero for k in range(steps) for s in range(steps + 1)],
        axis=0,
    ).astype(jnp.bfloat16)
    cols = (2 * SPAN + 1) * parts * slots
    block = (steps + 1) * parts
    col = lax.broadcasted_iota(jnp.int32, (LANES, cols), 1)
    particle = lax.rem(
        (row - SPAN + col // (parts * slots)) * parts + col % parts + 16 * LANES, LANES
    )
    spread = (particle == lax.broadcasted_iota(jnp.int32, (LANES, cols), 0)).astype(
        jnp.float32
    ).astype(jnp.bfloat16)
    from_where = nn(stack, spread)
    slot = lax.broadcasted_iota(jnp.int32, (block, cols), 1) // parts % slots
    kind = jnp.maximum(slot - history, 0)
    valid = jnp.zeros((block, cols), jnp.float32)
    for k in range(steps):
        valid = jnp.where(kind == k, from_where[k * block : (k + 1) * block], valid)

    for delta in FAR:
        @pl.when(inside(delta))
        def _():
            for copy in w_arrivals(delta):
                copy.wait_recv()
    old_in.wait()
    new_in.wait()

    pick = jnp.broadcast_to(valid[moments:, None, :], (parts, slots, cols)).reshape(parts * slots, cols)
    same = lax.broadcasted_iota(jnp.int32, (parts * slots, cols), 1) // parts % slots == lax.rem(
        lax.broadcasted_iota(jnp.int32, (parts * slots, cols), 0), slots
    )
    pick = jnp.where(same, pick, 0.0).astype(jnp.bfloat16)
    for c in range(0, 2 * key_width, 256):
        piece = window[:, :, c : c + 256].reshape(cols, 256)
        out_ref[:, c : c + 256] = nn(pick, piece).astype(jnp.bfloat16)

    at = pl.multiple_of(my_head * HEAD_DIM, HEAD_DIM)
    keys = window[:, :, pl.ds(at, HEAD_DIM)].reshape(cols, HEAD_DIM)
    vals = window[:, :, pl.ds(pl.multiple_of(at + key_width, HEAD_DIM), HEAD_DIM)].reshape(
        cols, HEAD_DIM
    )
    allowed = jnp.concatenate([valid[:moments]] * own, axis=0) > 0.5
    score = jnp.where(allowed, nt(q_all[column], keys) * factor, FLOOR)
    peak = jnp.max(score, axis=1, keepdims=True)
    weight = jnp.where(allowed, jnp.exp2(score - peak), 0.0)
    total = jnp.sum(weight, axis=1, keepdims=True)
    summed = nn(weight.astype(jnp.bfloat16), vals)

    for o in range(1, n_ctx):
        source = lax.rem(column + o, n_ctx)
        for copy in p_copies(source, source):
            copy.wait_recv()
    peaks, totals, scales, sums = [peak], [total], [1.0], [summed]
    for o in range(n_ctx):
        source = lax.rem(column + o, n_ctx)
        codes = part[column] if o == 0 else got[source]
        tile = part_stats[column] if o == 0 else got_stats[source]
        stats = jnp.transpose(
            jnp.concatenate([tile, jnp.zeros((LANES - 8, LANES), jnp.float32)], axis=0)
        )[:rows]
        peaks.append(stats[:, 0:1])
        totals.append(stats[:, 1:2])
        scales.append(stats[:, 2:3] * (1.0 / CODES))
        sums.append(codes.astype(jnp.int32).astype(jnp.float32))
    highest = functools.reduce(jnp.maximum, peaks)
    bottom, top = 0.0, 0.0
    for m, l, g, s in zip(peaks, totals, scales, sums):
        scale = jnp.exp2(m - highest)
        bottom = bottom + l * scale
        top = top + s * (g * scale)
    result = top / bottom
    for h in range(own):
        for s in range(steps):
            at = h * moments + s * parts
            att_ref[s, :, h * HEAD_DIM : (h + 1) * HEAD_DIM] = result[at : at + parts]

    q_copy(pair, column, r_send.at[column]).wait_send()
    for i in order:
        for peer in same_side(i):
            q_copy(peer, column, q_send.at[peer]).wait_send()
            q_copy(pair, peer, r_send.at[peer]).wait_send()
    for o in range(1, n_ctx):
        peer = lax.rem(column + o, n_ctx)
        for copy in p_copies(peer, column):
            copy.wait_send()
    for delta in FAR:
        @pl.when(inside(delta))
        def _():
            a_copy(delta).wait_send()
            for copy in w_copies(delta):
                copy.wait_send()


def solution(mesh):
    n_ctx, n_dom = mesh.shape["ctx"], mesh.shape["dom"]

    def shards(prompt_kv, suffix_kv, new_kv, queries, ancestors):
        parts, history, width = suffix_kv.shape
        steps = queries.shape[0]
        key_heads = width // (2 * HEAD_DIM)
        slots = history + steps
        positions = prompt_kv.shape[0]
        own = HEADS // n_ctx
        rows = own * steps * parts
        old = jnp.transpose(suffix_kv, (1, 0, 2)).reshape(history * parts, width)
        new = new_kv.reshape(steps * parts, width)
        anywhere = pl.BlockSpec(memory_space=pl.ANY)
        vmem = pl.BlockSpec(memory_space=pltpu.VMEM)
        dma = pltpu.SemaphoreType.DMA
        attended, suffix_out = pl.pallas_call(
            functools.partial(kernel, n_ctx, n_dom, key_heads, steps, history),
            out_shape=(
                jax.ShapeDtypeStruct((steps, parts, own * HEAD_DIM), jnp.float32),
                jax.ShapeDtypeStruct((parts * slots, width), jnp.bfloat16),
            ),
            in_specs=[anywhere] * 5,
            out_specs=(vmem, vmem),
            scratch_shapes=[
                pltpu.VMEM((key_heads, positions, HEAD_DIM), jnp.bfloat16),
                pltpu.VMEM((key_heads, positions, HEAD_DIM), jnp.bfloat16),
                pltpu.VMEM((steps, parts, own * HEAD_DIM), jnp.bfloat16),
                pltpu.VMEM((steps, parts), jnp.int32),
                pltpu.VMEM((n_ctx, rows, HEAD_DIM), jnp.bfloat16),
                pltpu.VMEM((n_ctx, rows, HEAD_DIM), jnp.int16),
                pltpu.VMEM((n_ctx, rows, HEAD_DIM), jnp.int16),
                pltpu.VMEM((n_ctx, 8, LANES), jnp.float32),
                pltpu.VMEM((n_ctx, 8, LANES), jnp.float32),
                pltpu.VMEM((2 * SPAN + 1, parts * slots, width), jnp.bfloat16),
                pltpu.VMEM((2 * SPAN + 1, 8, LANES), jnp.int32),
                dma((key_heads, 2)), dma((4,)),
                *[dma((n_ctx,))] * 7,
                *[dma((2 * SPAN + 1,))] * 6,
            ],
            compiler_params=pltpu.CompilerParams(
                collective_id=0, has_side_effects=True, vmem_limit_bytes=60 * 1024 * 1024
            ),
            cost_estimate=pl.CostEstimate(
                flops=4 * HEADS * steps * parts * positions * HEAD_DIM,
                bytes_accessed=4 * positions * width,
                transcendentals=HEADS * steps * parts * positions,
            ),
        )(prompt_kv, old, new, queries, ancestors)
        return attended, suffix_out.reshape(parts, slots, width)

    return jax.shard_map(
        shards,
        mesh=mesh,
        in_specs=(
            P("ctx", None),
            P("dom", None, None),
            P(None, "dom", None),
            P(None, "dom", "ctx"),
            P(None, "dom"),
        ),
        out_specs=(P(None, "dom", "ctx"), P("dom", None, None)),
        check_vma=False,
    )
```

```python
import functools

import jax
import jax.numpy as jnp
from jax import lax
from jax.experimental import pallas as pl
from jax.experimental.pallas import tpu as pltpu
from jax.sharding import PartitionSpec as P

HEADS = 32
HEAD_DIM = 128
MESH = pl.DeviceIdType.MESH
LOG2E = 1.4426950408889634
FLOOR = -1e30
LANES = 128
CODES = 32767.0
TINY = 1e-30
SPAN = 2
FAR = (-1, 1, -2, 2)


def nt(a, b):
    return lax.dot_general(a, b, (((1,), (1,)), ((), ())), preferred_element_type=jnp.float32)


def nn(a, b):
    return jnp.dot(a, b, preferred_element_type=jnp.float32)


def kernel(
    n_ctx, n_dom, key_heads, steps, history,
    kv_ref, old_ref, new_ref, q_ref, anc_ref,
    att_ref, out_ref,
    k_buf, v_buf, q_raw, anc_raw, q_all, part, got, part_stats, got_stats, window, anc_win,
    kv_sem, in_sem, q_send, q_recv, p_send, p_recv, t_send, t_recv,
    w_send, w_recv, n_send, n_recv, a_send, a_recv,
):
    column = lax.axis_index("ctx")
    row = lax.axis_index("dom")
    own = HEADS // n_ctx
    members = n_ctx // key_heads
    my_head = column // members
    my_member = column % members
    parts = q_ref.shape[1]
    slots = history + steps
    moments = steps * parts
    rows = own * moments
    key_width = key_heads * HEAD_DIM
    factor = LOG2E / HEAD_DIM**0.5

    pair = column + 1 - 2 * (column % 2)
    order = [0] + list(range(1, key_heads))

    q_in = pltpu.make_async_copy(q_ref, q_raw, in_sem.at[0])
    anc_in = pltpu.make_async_copy(anc_ref, anc_raw, in_sem.at[1])
    q_in.start()
    anc_in.start()
    barrier = pltpu.get_barrier_semaphore()
    for o in range(1, n_ctx):
        pl.semaphore_signal(
            barrier, inc=1, device_id={"ctx": lax.rem(column + o, n_ctx)}, device_id_type=MESH
        )

    def inside(delta):
        return (row + delta >= 0) & (row + delta < n_dom)

    for delta in FAR:
        @pl.when(inside(delta))
        def _():
            pl.semaphore_signal(barrier, inc=1, device_id={"dom": row + delta}, device_id_type=MESH)

    def head_at(i):
        e, bit = my_head, 1
        while bit < key_heads:
            if i & bit:
                e = e + bit - 2 * bit * (my_head // bit % 2)
            bit *= 2
        return e

    def same_side(i):
        e = head_at(i)
        half = members // 2
        mine = my_member // 2
        first = 1 if i == 0 else 0
        return [
            e * members + 2 * lax.rem(mine + o, half) + my_member % 2 for o in range(first, half)
        ]

    def loads(i):
        e = head_at(i)
        at = pl.multiple_of(e * HEAD_DIM, HEAD_DIM)
        return (
            pltpu.make_async_copy(kv_ref.at[:, pl.ds(at, HEAD_DIM)], k_buf.at[i], kv_sem.at[i, 0]),
            pltpu.make_async_copy(
                kv_ref.at[:, pl.ds(at + key_width, HEAD_DIM)], v_buf.at[i], kv_sem.at[i, 1]
            ),
        )

    old_rows, new_rows = old_ref.shape[0], new_ref.shape[0]
    old_in = pltpu.make_async_copy(old_ref, window.at[SPAN, pl.ds(0, old_rows)], in_sem.at[2])
    new_in = pltpu.make_async_copy(
        new_ref, window.at[SPAN, pl.ds(old_rows, new_rows)], in_sem.at[3]
    )
    for i in order:
        for copy in loads(i):
            copy.start()
    old_in.start()
    new_in.start()

    q_in.wait()
    anc_in.wait()
    wide = jnp.concatenate([q_raw[s].astype(jnp.float32) for s in range(steps)], axis=0)
    mine = jnp.concatenate(
        [wide[:, h * HEAD_DIM : (h + 1) * HEAD_DIM] for h in range(own)], axis=0
    ).astype(jnp.bfloat16)
    q_all[column] = mine
    lane = lax.broadcasted_iota(jnp.int32, (steps, LANES), 1)
    tile = jnp.full((steps, LANES), -1, jnp.int32)
    anc = anc_raw[...]
    for p in range(parts):
        tile = jnp.where(lane == lax.rem(row * parts + p, LANES), anc[:, p : p + 1], tile)
    anc_win[SPAN] = jnp.concatenate([tile, jnp.full((8 - steps, LANES), -1, jnp.int32)], axis=0)
    for delta in FAR:
        @pl.when(jnp.logical_not(inside(delta)))
        def _():
            anc_win[SPAN + delta] = jnp.full((8, LANES), -1, jnp.int32)
            window[SPAN + delta] = jnp.zeros(window.shape[1:], window.dtype)

    near = jnp.minimum(row, SPAN) + jnp.minimum(n_dom - 1 - row, SPAN)
    pl.semaphore_wait(barrier, n_ctx - 1 + near)

    def q_copy(peer, source, sems):
        return pltpu.make_async_remote_copy(
            src_ref=q_all.at[source], dst_ref=q_all.at[source],
            send_sem=sems, recv_sem=q_recv.at[source],
            device_id={"ctx": peer}, device_id_type=MESH,
        )

    def other(peer):
        return peer + 1 - 2 * (peer % 2)

    def arrive(i):
        for source in same_side(i):
            q_copy(source, source, q_send.at[source]).wait_recv()

    q_copy(pair, column, q_send.at[pair]).start()
    for i in order:
        for peer in same_side(i):
            q_copy(peer, column, q_send.at[peer]).start()
            q_copy(other(peer), column, q_send.at[other(peer)]).start()

    def w_pieces(delta, at, sent, landed):
        return [
            pltpu.make_async_remote_copy(
                src_ref=source, dst_ref=window.at[SPAN + at, pl.ds(first, source.shape[0])],
                send_sem=send.at[SPAN + sent], recv_sem=recv.at[SPAN + landed],
                device_id={"dom": row + delta}, device_id_type=MESH,
            )
            for source, first, send, recv in (
                (old_ref, 0, w_send, w_recv), (new_ref, old_rows, n_send, n_recv)
            )
        ]

    def w_copies(delta):
        return w_pieces(delta, -delta, delta, -delta)

    def w_arrivals(delta):
        return w_pieces(delta, delta, -delta, delta)

    def a_copy(delta):
        return pltpu.make_async_remote_copy(
            src_ref=anc_win.at[SPAN], dst_ref=anc_win.at[SPAN - delta],
            send_sem=a_send.at[SPAN + delta], recv_sem=a_recv.at[SPAN - delta],
            device_id={"dom": row + delta}, device_id_type=MESH,
        )

    def a_arrival(delta):
        return pltpu.make_async_remote_copy(
            src_ref=anc_win.at[SPAN], dst_ref=anc_win.at[SPAN + delta],
            send_sem=a_send.at[SPAN - delta], recv_sem=a_recv.at[SPAN + delta],
            device_id={"dom": row + delta}, device_id_type=MESH,
        )

    for delta in FAR:
        @pl.when(inside(delta))
        def _():
            a_copy(delta).start()
            for copy in w_copies(delta):
                copy.start()

    def p_copies(peer, source):
        return [
            pltpu.make_async_remote_copy(
                src_ref=mine.at[peer], dst_ref=theirs.at[source],
                send_sem=send.at[peer], recv_sem=recv.at[source],
                device_id={"ctx": peer}, device_id_type=MESH,
            )
            for mine, theirs, send, recv in (
                (part_stats, got_stats, t_send, t_recv), (part, got, p_send, p_recv)
            )
        ]

    def stats_tile(*columns):
        n = columns[0].shape[0]
        li = lax.broadcasted_iota(jnp.int32, (n, LANES), 1)
        both = jnp.zeros((n, LANES), jnp.float32)
        for at, value in enumerate(columns):
            both = jnp.where(li == at, value, both)
        turned = jnp.transpose(both)[:8]
        if n < LANES:
            turned = jnp.concatenate([turned, jnp.zeros((8, LANES - n), jnp.float32)], axis=1)
        return turned

    for n, i in enumerate(order):
        e = head_at(i)
        for copy in loads(i):
            copy.wait()
        arrive(i)
        for o in range(members // 2):
            source = e * members + 2 * o + pair % 2
            q_copy(source, source, q_send.at[source]).wait_recv()
        q = q_all[pl.ds(e * members, members)].reshape(members * rows, HEAD_DIM)
        score = nt(q, k_buf[i])
        peak = jnp.max(score, axis=1, keepdims=True) * factor
        weight = jnp.exp2(score * factor - peak)
        total = jnp.sum(weight, axis=1, keepdims=True)
        summed = nn(weight.astype(jnp.bfloat16), v_buf[i])
        largest = jnp.max(jnp.abs(summed), axis=1, keepdims=True)
        coded = jnp.round(summed * (CODES / jnp.maximum(largest, TINY))).astype(jnp.int32)
        coded = coded.astype(jnp.int16)
        for m in range(members):
            peer = e * members + m
            cut = slice(m * rows, (m + 1) * rows)
            part[peer] = coded[cut]
            part_stats[peer] = stats_tile(peak[cut], total[cut], largest[cut])
            if i == 0:
                @pl.when(m != my_member)
                def _():
                    for copy in p_copies(peer, column):
                        copy.start()
            else:
                for copy in p_copies(peer, column):
                    copy.start()

    for delta in FAR:
        @pl.when(inside(delta))
        def _():
            a_arrival(delta).wait_recv()
    known = anc_win[0]
    for w in range(1, 2 * SPAN + 1):
        known = jnp.maximum(known, anc_win[w])
    known = jnp.where(known >= 0, known & (LANES - 1), -1)
    q_id = lax.broadcasted_iota(jnp.int32, (LANES, LANES), 0)
    one = lax.broadcasted_iota(jnp.int32, (parts, LANES), 1) == (
        row * parts + lax.broadcasted_iota(jnp.int32, (parts, LANES), 0)
    ) & (LANES - 1)
    one = one.astype(jnp.float32)
    zero = jnp.zeros_like(one)
    origin = {}
    for k in range(steps - 1, -1, -1):
        origin[k, k] = one
        start = [origin[s, k + 1] for s in range(k + 1, steps + 1) if s != k + 1] + [one]
        names = list(range(k + 2, steps + 1)) + [k + 1]
        turn = (known[k : k + 1, :] == q_id).astype(jnp.float32).astype(jnp.bfloat16)
        moved = nt(jnp.concatenate(start, axis=0).astype(jnp.bfloat16), turn)
        for n, s in enumerate(names):
            origin[s, k] = moved[n * parts : (n + 1) * parts]
    stack = jnp.concatenate(
        [origin.get((s, k), zero) if s >= k else zero for k in range(steps) for s in range(steps + 1)],
        axis=0,
    ).astype(jnp.bfloat16)
    cols = (2 * SPAN + 1) * parts * slots
    block = (steps + 1) * parts
    p_bits, s_bits = parts.bit_length() - 1, slots.bit_length() - 1
    col = lax.broadcasted_iota(jnp.int32, (1, cols), 1)
    particle = ((row - SPAN + (col >> (p_bits + s_bits))) * parts + (col & (parts - 1))) & (LANES - 1)
    slot = (col >> p_bits) & (slots - 1)
    spread = (particle == lax.broadcasted_iota(jnp.int32, (LANES, cols), 0)).astype(
        jnp.float32
    ).astype(jnp.bfloat16)
    from_where = nn(stack, spread)
    kind = jnp.maximum(slot - history, 0)
    valid = jnp.zeros((block, cols), jnp.float32)
    for k in range(steps):
        valid = jnp.where(kind == k, from_where[k * block : (k + 1) * block], valid)

    for delta in FAR:
        @pl.when(inside(delta))
        def _():
            for copy in w_arrivals(delta):
                copy.wait_recv()
    old_in.wait()
    new_in.wait()

    pick = jnp.broadcast_to(valid[moments:, None, :], (parts, slots, cols)).reshape(parts * slots, cols)
    same = slot == lax.broadcasted_iota(jnp.int32, (parts * slots, 1), 0) & (slots - 1)
    pick = jnp.where(same, pick, 0.0).astype(jnp.bfloat16)
    for c in range(0, 2 * key_width, 256):
        piece = window[:, :, c : c + 256].reshape(cols, 256)
        out_ref[:, c : c + 256] = nn(pick, piece).astype(jnp.bfloat16)

    at = pl.multiple_of(my_head * HEAD_DIM, HEAD_DIM)
    keys = window[:, :, pl.ds(at, HEAD_DIM)].reshape(cols, HEAD_DIM)
    vals = window[:, :, pl.ds(pl.multiple_of(at + key_width, HEAD_DIM), HEAD_DIM)].reshape(
        cols, HEAD_DIM
    )
    allowed = jnp.concatenate([valid[:moments]] * own, axis=0) > 0.5
    score = jnp.where(allowed, nt(q_all[column], keys) * factor, FLOOR)
    peak = jnp.max(score, axis=1, keepdims=True)
    weight = jnp.where(allowed, jnp.exp2(score - peak), 0.0)
    total = jnp.sum(weight, axis=1, keepdims=True)
    summed = nn(weight.astype(jnp.bfloat16), vals)

    for o in range(1, n_ctx):
        source = lax.rem(column + o, n_ctx)
        for copy in p_copies(source, source):
            copy.wait_recv()
    sources = [lax.rem(column + o, n_ctx) for o in range(n_ctx)]
    peaks, totals, scales, sums = [peak], [total], [1.0], [summed]
    group = LANES // 8
    for first in range(0, n_ctx, group):
        some = range(first, min(first + group, n_ctx))
        tiles = [part_stats[column] if o == 0 else got_stats[sources[o]] for o in some]
        if len(tiles) < group:
            tiles.append(jnp.zeros((LANES - 8 * len(tiles), LANES), jnp.float32))
        stats = jnp.transpose(jnp.concatenate(tiles, axis=0))[:rows]
        for n, o in enumerate(some):
            codes = part[column] if o == 0 else got[sources[o]]
            peaks.append(stats[:, 8 * n : 8 * n + 1])
            totals.append(stats[:, 8 * n + 1 : 8 * n + 2])
            scales.append(stats[:, 8 * n + 2 : 8 * n + 3] * (1.0 / CODES))
            sums.append(codes.astype(jnp.int32).astype(jnp.float32))
    highest = functools.reduce(jnp.maximum, peaks)
    bottom, top = 0.0, 0.0
    for m, l, g, s in zip(peaks, totals, scales, sums):
        scale = jnp.exp2(m - highest)
        bottom = bottom + l * scale
        top = top + s * (g * scale)
    result = top / bottom
    for h in range(own):
        for s in range(steps):
            at = h * moments + s * parts
            att_ref[s, :, h * HEAD_DIM : (h + 1) * HEAD_DIM] = result[at : at + parts]

    q_copy(pair, column, q_send.at[pair]).wait_send()
    for i in order:
        for peer in same_side(i):
            q_copy(peer, column, q_send.at[peer]).wait_send()
            q_copy(other(peer), column, q_send.at[other(peer)]).wait_send()
    for o in range(1, n_ctx):
        peer = lax.rem(column + o, n_ctx)
        for copy in p_copies(peer, column):
            copy.wait_send()
    for delta in FAR:
        @pl.when(inside(delta))
        def _():
            a_copy(delta).wait_send()
            for copy in w_copies(delta):
                copy.wait_send()


def solution(mesh):
    n_ctx, n_dom = mesh.shape["ctx"], mesh.shape["dom"]

    def shards(prompt_kv, suffix_kv, new_kv, queries, ancestors):
        parts, history, width = suffix_kv.shape
        steps = queries.shape[0]
        key_heads = width // (2 * HEAD_DIM)
        slots = history + steps
        positions = prompt_kv.shape[0]
        own = HEADS // n_ctx
        rows = own * steps * parts
        old = jnp.transpose(suffix_kv, (1, 0, 2)).reshape(history * parts, width)
        new = new_kv.reshape(steps * parts, width)
        hbm = pl.BlockSpec(memory_space=pltpu.HBM)
        vmem = pl.BlockSpec(memory_space=pltpu.VMEM)
        dma = pltpu.SemaphoreType.DMA
        attended, suffix_out = pl.pallas_call(
            functools.partial(kernel, n_ctx, n_dom, key_heads, steps, history),
            out_shape=(
                jax.ShapeDtypeStruct((steps, parts, own * HEAD_DIM), jnp.float32),
                jax.ShapeDtypeStruct((parts * slots, width), jnp.bfloat16),
            ),
            in_specs=[hbm] * 5,
            out_specs=(vmem, vmem),
            scratch_shapes=[
                pltpu.VMEM((key_heads, positions, HEAD_DIM), jnp.bfloat16),
                pltpu.VMEM((key_heads, positions, HEAD_DIM), jnp.bfloat16),
                pltpu.VMEM((steps, parts, own * HEAD_DIM), jnp.bfloat16),
                pltpu.VMEM((steps, parts), jnp.int32),
                pltpu.VMEM((n_ctx, rows, HEAD_DIM), jnp.bfloat16),
                pltpu.VMEM((n_ctx, rows, HEAD_DIM), jnp.int16),
                pltpu.VMEM((n_ctx, rows, HEAD_DIM), jnp.int16),
                pltpu.VMEM((n_ctx, 8, LANES), jnp.float32),
                pltpu.VMEM((n_ctx, 8, LANES), jnp.float32),
                pltpu.VMEM((2 * SPAN + 1, parts * slots, width), jnp.bfloat16),
                pltpu.VMEM((2 * SPAN + 1, 8, LANES), jnp.int32),
                dma((key_heads, 2)), dma((4,)),
                *[dma((n_ctx,))] * 6,
                *[dma((2 * SPAN + 1,))] * 6,
            ],
            compiler_params=pltpu.CompilerParams(
                collective_id=0, has_side_effects=True, vmem_limit_bytes=60 * 1024 * 1024
            ),
            cost_estimate=pl.CostEstimate(
                flops=4 * HEADS * steps * parts * positions * HEAD_DIM,
                bytes_accessed=4 * positions * width,
                transcendentals=HEADS * steps * parts * positions,
            ),
        )(prompt_kv, old, new, queries, ancestors)
        return attended, suffix_out.reshape(parts, slots, width)

    return jax.shard_map(
        shards,
        mesh=mesh,
        in_specs=(
            P("ctx", None),
            P("dom", None, None),
            P(None, "dom", None),
            P(None, "dom", "ctx"),
            P(None, "dom"),
        ),
        out_specs=(P(None, "dom", "ctx"), P("dom", None, None)),
        check_vma=False,
    )
```

```python
import functools

import jax
import jax.numpy as jnp
from jax import lax
from jax.experimental import pallas as pl
from jax.experimental.pallas import tpu as pltpu
from jax.sharding import PartitionSpec as P

HEADS = 32
HEAD_DIM = 128
MESH = pl.DeviceIdType.MESH
LOG2E = 1.4426950408889634
FLOOR = -1e30
LANES = 128
CODES = 32767.0
TINY = 1e-30
SPAN = 2
FAR = (-1, 1, -2, 2)


def nt(a, b):
    return lax.dot_general(a, b, (((1,), (1,)), ((), ())), preferred_element_type=jnp.float32)


def nn(a, b):
    return jnp.dot(a, b, preferred_element_type=jnp.float32)


def kernel(
    n_ctx, n_dom, key_heads, steps, history,
    kv_ref, old_ref, new_ref, q_ref, anc_ref,
    att_ref, suffix_out,
    k_buf, v_buf, q_raw, anc_raw, q_all, part, got, part_stats, got_stats, window, anc_win, out_ref,
    kv_sem, in_sem, q_send, q_recv, p_send, p_recv, t_send, t_recv,
    w_send, w_recv, n_send, n_recv, a_send, a_recv,
):
    column = lax.axis_index("ctx")
    row = lax.axis_index("dom")
    own = HEADS // n_ctx
    members = n_ctx // key_heads
    my_head = column // members
    my_member = column % members
    parts = q_ref.shape[1]
    slots = history + steps
    moments = steps * parts
    rows = own * moments
    key_width = key_heads * HEAD_DIM
    factor = LOG2E / HEAD_DIM**0.5

    pair = column + 1 - 2 * (column % 2)
    order = [0] + list(range(1, key_heads))

    q_in = pltpu.make_async_copy(q_ref, q_raw, in_sem.at[0])
    anc_in = pltpu.make_async_copy(anc_ref, anc_raw, in_sem.at[1])
    q_in.start()
    anc_in.start()
    barrier = pltpu.get_barrier_semaphore()
    for o in range(1, n_ctx):
        pl.semaphore_signal(
            barrier, inc=1, device_id={"ctx": lax.rem(column + o, n_ctx)}, device_id_type=MESH
        )

    def inside(delta):
        return (row + delta >= 0) & (row + delta < n_dom)

    for delta in FAR:
        @pl.when(inside(delta))
        def _():
            pl.semaphore_signal(barrier, inc=1, device_id={"dom": row + delta}, device_id_type=MESH)

    def head_at(i):
        e, bit = my_head, 1
        while bit < key_heads:
            if i & bit:
                e = e + bit - 2 * bit * (my_head // bit % 2)
            bit *= 2
        return e

    def same_side(i):
        e = head_at(i)
        half = members // 2
        mine = my_member // 2
        first = 1 if i == 0 else 0
        return [
            e * members + 2 * lax.rem(mine + o, half) + my_member % 2 for o in range(first, half)
        ]

    def loads(i):
        e = head_at(i)
        at = pl.multiple_of(e * HEAD_DIM, HEAD_DIM)
        return (
            pltpu.make_async_copy(kv_ref.at[:, pl.ds(at, HEAD_DIM)], k_buf.at[i], kv_sem.at[i, 0]),
            pltpu.make_async_copy(
                kv_ref.at[:, pl.ds(at + key_width, HEAD_DIM)], v_buf.at[i], kv_sem.at[i, 1]
            ),
        )

    old_rows, new_rows = old_ref.shape[0], new_ref.shape[0]
    old_in = pltpu.make_async_copy(old_ref, window.at[SPAN, pl.ds(0, old_rows)], in_sem.at[2])
    new_in = pltpu.make_async_copy(
        new_ref, window.at[SPAN, pl.ds(old_rows, new_rows)], in_sem.at[3]
    )
    for i in order:
        for copy in loads(i):
            copy.start()
    old_in.start()
    new_in.start()

    q_in.wait()
    anc_in.wait()
    wide = jnp.concatenate([q_raw[s].astype(jnp.float32) for s in range(steps)], axis=0)
    mine = jnp.concatenate(
        [wide[:, h * HEAD_DIM : (h + 1) * HEAD_DIM] for h in range(own)], axis=0
    ).astype(jnp.bfloat16)
    q_all[column] = mine
    lane = lax.broadcasted_iota(jnp.int32, (steps, LANES), 1)
    tile = jnp.full((steps, LANES), -1, jnp.int32)
    anc = anc_raw[...]
    for p in range(parts):
        tile = jnp.where(lane == lax.rem(row * parts + p, LANES), anc[:, p : p + 1], tile)
    anc_win[SPAN] = jnp.concatenate([tile, jnp.full((8 - steps, LANES), -1, jnp.int32)], axis=0)
    for delta in FAR:
        @pl.when(jnp.logical_not(inside(delta)))
        def _():
            anc_win[SPAN + delta] = jnp.full((8, LANES), -1, jnp.int32)
            window[SPAN + delta] = jnp.zeros(window.shape[1:], window.dtype)

    near = jnp.minimum(row, SPAN) + jnp.minimum(n_dom - 1 - row, SPAN)
    pl.semaphore_wait(barrier, n_ctx - 1 + near)

    def q_copy(peer, source, sems):
        return pltpu.make_async_remote_copy(
            src_ref=q_all.at[source], dst_ref=q_all.at[source],
            send_sem=sems, recv_sem=q_recv.at[source],
            device_id={"ctx": peer}, device_id_type=MESH,
        )

    def other(peer):
        return peer + 1 - 2 * (peer % 2)

    def arrive(i):
        for source in same_side(i):
            q_copy(source, source, q_send.at[source]).wait_recv()

    q_copy(pair, column, q_send.at[pair]).start()
    for i in order:
        for peer in same_side(i):
            q_copy(peer, column, q_send.at[peer]).start()
            q_copy(other(peer), column, q_send.at[other(peer)]).start()

    def w_pieces(delta, at, sent, landed):
        return [
            pltpu.make_async_remote_copy(
                src_ref=source, dst_ref=window.at[SPAN + at, pl.ds(first, source.shape[0])],
                send_sem=send.at[SPAN + sent], recv_sem=recv.at[SPAN + landed],
                device_id={"dom": row + delta}, device_id_type=MESH,
            )
            for source, first, send, recv in (
                (old_ref, 0, w_send, w_recv), (new_ref, old_rows, n_send, n_recv)
            )
        ]

    def w_copies(delta):
        return w_pieces(delta, -delta, delta, -delta)

    def w_arrivals(delta):
        return w_pieces(delta, delta, -delta, delta)

    def a_copy(delta):
        return pltpu.make_async_remote_copy(
            src_ref=anc_win.at[SPAN], dst_ref=anc_win.at[SPAN - delta],
            send_sem=a_send.at[SPAN + delta], recv_sem=a_recv.at[SPAN - delta],
            device_id={"dom": row + delta}, device_id_type=MESH,
        )

    def a_arrival(delta):
        return pltpu.make_async_remote_copy(
            src_ref=anc_win.at[SPAN], dst_ref=anc_win.at[SPAN + delta],
            send_sem=a_send.at[SPAN - delta], recv_sem=a_recv.at[SPAN + delta],
            device_id={"dom": row + delta}, device_id_type=MESH,
        )

    for delta in FAR:
        @pl.when(inside(delta))
        def _():
            a_copy(delta).start()
            for copy in w_copies(delta):
                copy.start()

    def p_copies(peer, source):
        return [
            pltpu.make_async_remote_copy(
                src_ref=mine.at[peer], dst_ref=theirs.at[source],
                send_sem=send.at[peer], recv_sem=recv.at[source],
                device_id={"ctx": peer}, device_id_type=MESH,
            )
            for mine, theirs, send, recv in (
                (part_stats, got_stats, t_send, t_recv), (part, got, p_send, p_recv)
            )
        ]

    def stats_tile(*columns):
        n = columns[0].shape[0]
        li = lax.broadcasted_iota(jnp.int32, (n, LANES), 1)
        both = jnp.zeros((n, LANES), jnp.float32)
        for at, value in enumerate(columns):
            both = jnp.where(li == at, value, both)
        turned = jnp.transpose(both)[:8]
        if n < LANES:
            turned = jnp.concatenate([turned, jnp.zeros((8, LANES - n), jnp.float32)], axis=1)
        return turned

    for n, i in enumerate(order):
        e = head_at(i)
        for copy in loads(i):
            copy.wait()
        arrive(i)
        for o in range(members // 2):
            source = e * members + 2 * o + pair % 2
            q_copy(source, source, q_send.at[source]).wait_recv()
        q = q_all[pl.ds(e * members, members)].reshape(members * rows, HEAD_DIM)
        score = nt(q, k_buf[i])
        peak = jnp.max(score, axis=1, keepdims=True) * factor
        weight = jnp.exp2(score * factor - peak)
        total = jnp.sum(weight, axis=1, keepdims=True)
        summed = nn(weight.astype(jnp.bfloat16), v_buf[i])
        largest = jnp.max(jnp.abs(summed), axis=1, keepdims=True)
        coded = jnp.round(summed * (CODES / jnp.maximum(largest, TINY))).astype(jnp.int32)
        coded = coded.astype(jnp.int16)
        for m in range(members):
            peer = e * members + m
            cut = slice(m * rows, (m + 1) * rows)
            part[peer] = coded[cut]
            part_stats[peer] = stats_tile(peak[cut], total[cut], largest[cut])
            if i == 0:
                @pl.when(m != my_member)
                def _():
                    for copy in p_copies(peer, column):
                        copy.start()
            else:
                for copy in p_copies(peer, column):
                    copy.start()

    for delta in FAR:
        @pl.when(inside(delta))
        def _():
            a_arrival(delta).wait_recv()
    known = anc_win[0]
    for w in range(1, 2 * SPAN + 1):
        known = jnp.maximum(known, anc_win[w])
    known = jnp.where(known >= 0, known & (LANES - 1), -1)
    q_id = lax.broadcasted_iota(jnp.int32, (LANES, LANES), 0)
    one = lax.broadcasted_iota(jnp.int32, (parts, LANES), 1) == (
        row * parts + lax.broadcasted_iota(jnp.int32, (parts, LANES), 0)
    ) & (LANES - 1)
    one = one.astype(jnp.float32)
    zero = jnp.zeros_like(one)
    origin = {}
    for k in range(steps - 1, -1, -1):
        origin[k, k] = one
        start = [origin[s, k + 1] for s in range(k + 1, steps + 1) if s != k + 1] + [one]
        names = list(range(k + 2, steps + 1)) + [k + 1]
        turn = (known[k : k + 1, :] == q_id).astype(jnp.float32).astype(jnp.bfloat16)
        moved = nt(jnp.concatenate(start, axis=0).astype(jnp.bfloat16), turn)
        for n, s in enumerate(names):
            origin[s, k] = moved[n * parts : (n + 1) * parts]
    stack = jnp.concatenate(
        [origin.get((s, k), zero) if s >= k else zero for k in range(steps) for s in range(steps + 1)],
        axis=0,
    ).astype(jnp.bfloat16)
    cols = (2 * SPAN + 1) * parts * slots
    block = (steps + 1) * parts
    p_bits, s_bits = parts.bit_length() - 1, slots.bit_length() - 1
    col = lax.broadcasted_iota(jnp.int32, (1, cols), 1)
    particle = ((row - SPAN + (col >> (p_bits + s_bits))) * parts + (col & (parts - 1))) & (LANES - 1)
    slot = (col >> p_bits) & (slots - 1)
    spread = (particle == lax.broadcasted_iota(jnp.int32, (LANES, cols), 0)).astype(
        jnp.float32
    ).astype(jnp.bfloat16)
    from_where = nn(stack, spread)
    kind = jnp.maximum(slot - history, 0)
    valid = jnp.zeros((block, cols), jnp.float32)
    for k in range(steps):
        valid = jnp.where(kind == k, from_where[k * block : (k + 1) * block], valid)

    for delta in FAR:
        @pl.when(inside(delta))
        def _():
            for copy in w_arrivals(delta):
                copy.wait_recv()
    old_in.wait()
    new_in.wait()

    pick = jnp.broadcast_to(valid[moments:, None, :], (parts, slots, cols)).reshape(parts * slots, cols)
    same = slot == lax.broadcasted_iota(jnp.int32, (parts * slots, 1), 0) & (slots - 1)
    pick = jnp.where(same, pick, 0.0).astype(jnp.bfloat16)
    for c in range(0, 2 * key_width, 256):
        piece = window[:, :, c : c + 256].reshape(cols, 256)
        out_ref[:, c : c + 256] = nn(pick, piece).astype(jnp.bfloat16)

    suffix_write = pltpu.make_async_copy(out_ref, suffix_out, in_sem.at[4])
    suffix_write.start()

    at = pl.multiple_of(my_head * HEAD_DIM, HEAD_DIM)
    keys = window[:, :, pl.ds(at, HEAD_DIM)].reshape(cols, HEAD_DIM)
    vals = window[:, :, pl.ds(pl.multiple_of(at + key_width, HEAD_DIM), HEAD_DIM)].reshape(
        cols, HEAD_DIM
    )
    allowed = jnp.concatenate([valid[:moments]] * own, axis=0) > 0.5
    score = jnp.where(allowed, nt(q_all[column], keys) * factor, FLOOR)
    peak = jnp.max(score, axis=1, keepdims=True)
    weight = jnp.where(allowed, jnp.exp2(score - peak), 0.0)
    total = jnp.sum(weight, axis=1, keepdims=True)
    summed = nn(weight.astype(jnp.bfloat16), vals)

    for o in range(1, n_ctx):
        source = lax.rem(column + o, n_ctx)
        for copy in p_copies(source, source):
            copy.wait_recv()
    sources = [lax.rem(column + o, n_ctx) for o in range(n_ctx)]
    peaks, totals, scales, sums = [peak], [total], [1.0], [summed]
    group = LANES // 8
    for first in range(0, n_ctx, group):
        some = range(first, min(first + group, n_ctx))
        tiles = [part_stats[column] if o == 0 else got_stats[sources[o]] for o in some]
        if len(tiles) < group:
            tiles.append(jnp.zeros((LANES - 8 * len(tiles), LANES), jnp.float32))
        stats = jnp.transpose(jnp.concatenate(tiles, axis=0))[:rows]
        for n, o in enumerate(some):
            codes = part[column] if o == 0 else got[sources[o]]
            peaks.append(stats[:, 8 * n : 8 * n + 1])
            totals.append(stats[:, 8 * n + 1 : 8 * n + 2])
            scales.append(stats[:, 8 * n + 2 : 8 * n + 3] * (1.0 / CODES))
            sums.append(codes.astype(jnp.int32).astype(jnp.float32))
    highest = functools.reduce(jnp.maximum, peaks)
    bottom, top = 0.0, 0.0
    for m, l, g, s in zip(peaks, totals, scales, sums):
        scale = jnp.exp2(m - highest)
        bottom = bottom + l * scale
        top = top + s * (g * scale)
    result = top / bottom
    for h in range(own):
        for s in range(steps):
            at = h * moments + s * parts
            att_ref[s, :, h * HEAD_DIM : (h + 1) * HEAD_DIM] = result[at : at + parts]

    q_copy(pair, column, q_send.at[pair]).wait_send()
    for i in order:
        for peer in same_side(i):
            q_copy(peer, column, q_send.at[peer]).wait_send()
            q_copy(other(peer), column, q_send.at[other(peer)]).wait_send()
    for o in range(1, n_ctx):
        peer = lax.rem(column + o, n_ctx)
        for copy in p_copies(peer, column):
            copy.wait_send()
    for delta in FAR:
        @pl.when(inside(delta))
        def _():
            a_copy(delta).wait_send()
            for copy in w_copies(delta):
                copy.wait_send()
    suffix_write.wait()


def solution(mesh):
    n_ctx, n_dom = mesh.shape["ctx"], mesh.shape["dom"]

    def shards(prompt_kv, suffix_kv, new_kv, queries, ancestors):
        parts, history, width = suffix_kv.shape
        steps = queries.shape[0]
        key_heads = width // (2 * HEAD_DIM)
        slots = history + steps
        positions = prompt_kv.shape[0]
        own = HEADS // n_ctx
        rows = own * steps * parts
        old = jnp.transpose(suffix_kv, (1, 0, 2)).reshape(history * parts, width)
        new = new_kv.reshape(steps * parts, width)
        hbm = pl.BlockSpec(memory_space=pltpu.HBM)
        vmem = pl.BlockSpec(memory_space=pltpu.VMEM)
        dma = pltpu.SemaphoreType.DMA
        attended, suffix_out = pl.pallas_call(
            functools.partial(kernel, n_ctx, n_dom, key_heads, steps, history),
            out_shape=(
                jax.ShapeDtypeStruct((steps, parts, own * HEAD_DIM), jnp.float32),
                jax.ShapeDtypeStruct((parts * slots, width), jnp.bfloat16),
            ),
            in_specs=[hbm] * 5,
            out_specs=(vmem, hbm),
            scratch_shapes=[
                pltpu.VMEM((key_heads, positions, HEAD_DIM), jnp.bfloat16),
                pltpu.VMEM((key_heads, positions, HEAD_DIM), jnp.bfloat16),
                pltpu.VMEM((steps, parts, own * HEAD_DIM), jnp.bfloat16),
                pltpu.VMEM((steps, parts), jnp.int32),
                pltpu.VMEM((n_ctx, rows, HEAD_DIM), jnp.bfloat16),
                pltpu.VMEM((n_ctx, rows, HEAD_DIM), jnp.int16),
                pltpu.VMEM((n_ctx, rows, HEAD_DIM), jnp.int16),
                pltpu.VMEM((n_ctx, 8, LANES), jnp.float32),
                pltpu.VMEM((n_ctx, 8, LANES), jnp.float32),
                pltpu.VMEM((2 * SPAN + 1, parts * slots, width), jnp.bfloat16),
                pltpu.VMEM((2 * SPAN + 1, 8, LANES), jnp.int32),
                pltpu.VMEM((parts * slots, width), jnp.bfloat16),
                dma((key_heads, 2)), dma((5,)),
                *[dma((n_ctx,))] * 6,
                *[dma((2 * SPAN + 1,))] * 6,
            ],
            compiler_params=pltpu.CompilerParams(
                collective_id=0, has_side_effects=True, vmem_limit_bytes=60 * 1024 * 1024
            ),
            cost_estimate=pl.CostEstimate(
                flops=4 * HEADS * steps * parts * positions * HEAD_DIM,
                bytes_accessed=4 * positions * width,
                transcendentals=HEADS * steps * parts * positions,
            ),
        )(prompt_kv, old, new, queries, ancestors)
        return attended, suffix_out.reshape(parts, slots, width)

    return jax.shard_map(
        shards,
        mesh=mesh,
        in_specs=(
            P("ctx", None),
            P("dom", None, None),
            P(None, "dom", None),
            P(None, "dom", "ctx"),
            P(None, "dom"),
        ),
        out_specs=(P(None, "dom", "ctx"), P("dom", None, None)),
        check_vma=False,
    )
```
